256 devices in a mesh: az: 32 (over x, y, core), rad: 8 (over z).
Axes of the slice: x: 4, y: 4, z: 8, core: 2. Of those that a mesh axis runs over, the one named last changes fastest.
Arguments:
- fields: float32 [2, 256, 8, 16384], P(None, 'rad', None, 'az'), may hold values from 0.1 to 2
- cycle_blocks: int32 [256, 1], P('rad'), may hold values from 0 to 31, as said below
- cycle_cells: int32 [256], P('rad'), may hold values from 0 to 511
- cycle_fracs: float32 [256], P('rad'), may hold values from 0 to 1
- coupling: float32 [2, 256], P(None, 'rad'), may hold values from 300 to 3000
Outputs:
- evolved: float32 [2, 256, 8, 16384], P(None, 'rad', None, 'az')
The draws below stay inside these ranges and needn't reach their ends.
Inputs may be any that keep to these rules, and one draw needn't show every extreme that they name: `cycle_blocks`: in each aligned block of 32 cycles (the cycles of one index of rad) no value is named by more than 2 cycles.
All inputs are finite; a program needn't handle non-finite values.
Results may differ from the reference program's by a relative error of at most 0.0003.
Values sent between devices are 32-bit elements; how exact they have to be, the bound alone decides.
A program may use at most 128 MiB of HBM per device.

```python
import math
import jax
import jax.numpy as jnp
from jax import lax

FL = 2
NZ = 8
RD = 32
AD = 512
NR = 256
NA = 16384
MOST = 2
N_AZ = 32
N_RAD = 8


def shear_profile(key):
    inner_key = jax.random.fold_in(key, 31)
    base = jax.random.randint(jax.random.fold_in(inner_key, 1), (), 0, N_AZ).astype(jnp.int32)
    group_ids = jnp.arange(N_RAD, dtype=jnp.int32)
    steps_out = N_RAD - 1 - group_ids
    run_of_group = jnp.maximum(1, MOST // (1 + steps_out * 3 // N_RAD)).astype(jnp.int32)
    runs_in_group = (RD + run_of_group - 1) // run_of_group
    runs_before = (jnp.cumsum(runs_in_group) - runs_in_group).astype(jnp.int32)
    cycle = jnp.arange(NR, dtype=jnp.int32)
    group = cycle // RD
    local = cycle % RD
    run_len = run_of_group[group]
    run_index = runs_before[group] + local // run_len
    blocks = ((base - run_index) % N_AZ).astype(jnp.int32)
    span = jnp.maximum(1, AD // run_len)
    noise = jax.random.randint(jax.random.fold_in(inner_key, 2), (NR,), 0, 1 << 20).astype(jnp.int32)
    jitter = noise % span
    cells = AD - 1 - local % run_len * AD // run_len - jitter
    cells = jnp.where(local == 0, AD - 1, cells)
    cells = jnp.where(local == RD - 1, 0, cells)
    return (blocks, jnp.clip(cells, 0, AD - 1).astype(jnp.int32))


def draw_cycle_blocks(key, part):
    blocks, cells = shear_profile(key)
    return blocks[:, None]


def draw_cycle_cells(key, part):
    blocks, cells = shear_profile(key)
    return cells


def block_levels(stream_key, extent, split, low, largest):
    gain, own = 1.0, jax.random.fold_in(stream_key, 6)
    for dim, shards_of in split:
        steps = jnp.exp(jax.random.uniform(jax.random.fold_in(own, dim), (shards_of,), jnp.float32, low / len(split), largest / len(split)))
        gain = gain * jnp.repeat(steps, extent[dim] // shards_of).reshape([-1 if axis == dim else 1 for axis in range(len(extent))])
    return gain


def setup_inputs(seed: int = 0) -> dict:
    arg_keys = jax.random.split(jax.random.key(seed), 6)
    fields = jnp.clip(jnp.exp(math.log(2.0) - 2.9957323 * jax.random.uniform(arg_keys[0], (FL, NR, NZ, NA), jnp.float32) ** block_levels(arg_keys[0], (FL, NR, NZ, NA), ((1, 8), (3, 32)), -0.2, 0.2)), 0.1, 2.0)
    cycle_blocks = draw_cycle_blocks(jax.random.fold_in(arg_keys[5], 71), 0)
    cycle_cells = draw_cycle_cells(jax.random.fold_in(arg_keys[5], 71), 0)
    cycle_fracs = jnp.clip(1.0 * jax.random.uniform(arg_keys[3], (NR,), jnp.float32) ** block_levels(arg_keys[3], (NR,), ((0, 8),), -0.2, 0.2), 0.0, 1.0)
    coupling = jnp.clip(jnp.exp(math.log(3000.0) - 2.3025851 * jax.random.uniform(arg_keys[4], (FL, NR), jnp.float32) ** block_levels(arg_keys[4], (FL, NR), ((1, 8),), -0.2, 0.2)), 300.0, 3000.0)
    return {"fields": fields, "cycle_blocks": cycle_blocks, "cycle_cells": cycle_cells, "cycle_fracs": cycle_fracs, "coupling": coupling}


def cycle_take(cycle, places):
    return jnp.take(cycle, places, axis=-1)

def reference(fields, cycle_blocks, cycle_cells, cycle_fracs, coupling):
    offset = AD * cycle_blocks[:, 0] + cycle_cells
    column = jnp.arange(NA, dtype=jnp.int32)
    near_place = ((column[None, :] - offset[:, None]) % NA).astype(jnp.int32)
    far_place = ((column[None, :] - offset[:, None] - 1) % NA).astype(jnp.int32)
    nearer = jax.vmap(cycle_take, in_axes=(1, 0), out_axes=1)(fields, near_place)
    farther = jax.vmap(cycle_take, in_axes=(1, 0), out_axes=1)(fields, far_place)
    weight = cycle_fracs[None, :, None, None]
    shifted = (1.0 - weight) * nearer + weight * farther
    zero_col = jnp.zeros((FL, 1), coupling.dtype)
    coupled = jnp.concatenate([zero_col, coupling[:, 1:]], axis=1)
    outer = jnp.concatenate([coupled[:, 1:], zero_col], axis=1)
    lower_band = -coupled
    main_band = 1.0 + coupled + outer
    upper_band = -outer
    right_side = shifted.reshape(FL, NR, NZ * NA)
    solved = lax.linalg.tridiagonal_solve(lower_band, main_band, upper_band, right_side)
    return solved.reshape(shifted.shape)
```

```python
import functools

import jax
import jax.numpy as jnp
from jax import lax
from jax.experimental import pallas as pl
from jax.experimental.pallas import tpu as pltpu
from jax.sharding import PartitionSpec as P

MESH = pl.DeviceIdType.MESH
LANES = 128


def kernel(
    n_az,
    n_rad,
    grid,
    fields,
    blocks,
    cells,
    fracs,
    coupling,
    out,
    recv1_0,
    recv1_1,
    send2_0,
    send2_1,
    recv2_0,
    recv2_1,
    solved,
    coup_all,
    rcoup,
    rcoup_s,
    u_s,
    v_s,
    zsend,
    zrecv_0,
    zrecv_1,
    p1_send,
    p1_recv,
    p2_send,
    p2_recv,
    z_send,
    z_recv,
    c_send,
    c_recv,
    l_sem,
    o_sem,
):
    recv1 = (recv1_0, recv1_1)
    send2 = (send2_0, send2_1)
    recv2 = (recv2_0, recv2_1)
    zrecv = (zrecv_0, zrecv_1)
    fluids, cycles, tiles, vertical, _ = fields.shape
    width = tiles * LANES
    plane = (tiles, vertical, LANES)
    _, ny, nc = grid
    a = lax.axis_index("az")
    k = lax.axis_index("rad")
    ax = a // (ny * nc)
    ay = (a // nc) % ny
    ac = a % nc

    def partner(step):
        x = (ax + step // (ny * nc)) % (n_az // (ny * nc))
        y = (ay + (step // nc) % ny) % ny
        c = (ac + step) % nc
        return (x * ny + y) * nc + c

    barrier = pltpu.get_barrier_semaphore()

    def greet(step, carry):
        pl.semaphore_signal(barrier, inc=1, device_id={"az": partner(step)}, device_id_type=MESH)
        return carry

    lax.fori_loop(1, n_az, greet, 0)
    for step in range(1, n_rad):
        pl.semaphore_signal(barrier, inc=1, device_id={"rad": (k + step) % n_rad}, device_id_type=MESH)
    pl.semaphore_wait(barrier, n_az - 1 + n_rad - 1)

    for f in range(fluids):

        def spread(step, carry, f=f):
            t = partner(step)
            pltpu.make_async_remote_copy(
                src_ref=fields.at[f, t],
                dst_ref=recv1[f].at[a],
                send_sem=p1_send.at[f],
                recv_sem=p1_recv.at[f],
                device_id={"az": t},
                device_id_type=MESH,
            ).start()
            return carry

        pltpu.make_async_copy(fields.at[f, a], recv1[f].at[a], p1_recv.at[f]).start()
        lax.fori_loop(1, n_az, spread, 0)
        if f == 0:
            coup_all[k] = coupling[...]
            for step in range(1, n_rad):
                pltpu.make_async_remote_copy(
                    src_ref=coupling,
                    dst_ref=coup_all.at[k],
                    send_sem=c_send,
                    recv_sem=c_recv,
                    device_id={"rad": (k + step) % n_rad},
                    device_id_type=MESH,
                ).start()

    part = coup_all.at[pl.ds(0, n_rad - 1)]
    pltpu.make_async_copy(part, part, c_recv).wait()
    pltpu.make_async_copy(part, part, c_send).wait()
    rcoup[...] = 1.0 / coup_all[...]
    to_scalar = pltpu.make_async_copy(rcoup, rcoup_s, l_sem)
    to_scalar.start()
    to_scalar.wait()

    def chain(block, carry):
        carry = list(carry)
        back = n_rad - 1 - block
        for i in range(cycles):
            j = cycles - 1 - i
            for f in range(fluids):
                u, flux, v, gain = carry[4 * f : 4 * f + 4]
                flux = flux + u
                u = u + flux * rcoup_s[block, f, i]
                u_s[f, block * cycles + i] = u
                v_s[f, back * cycles + j] = v
                gain = gain + v
                v = v + gain * rcoup_s[back, f, j]
                carry[4 * f : 4 * f + 4] = [u, flux, v, gain]
        return tuple(carry)

    one, zero = jnp.float32(1.0), jnp.float32(0.0)
    last = lax.fori_loop(0, n_rad, chain, (one, -one, one, zero) * fluids)
    scale = [1.0 / jnp.full(plane, last[4 * f] + last[4 * f + 1], jnp.float32) for f in range(fluids)]

    offset = width * blocks[a] + cells[a]
    shift = offset % LANES
    base = tiles * n_az - offset // LANES
    weight = fracs[a]
    lane = lax.broadcasted_iota(jnp.int32, (vertical, LANES), 1)
    near_keep = lane >= shift
    far_keep = lane >= shift + 1
    far_shift = (shift + 1) % LANES

    def rotated(f, t):
        near, far = [], []
        for j in range(-1, tiles):
            n = (base + tiles * t + j + tiles * n_az) % (tiles * n_az)
            tile = recv1[f][n // tiles, n % tiles]
            near.append(pltpu.roll(tile, shift, 1))
            far.append(pltpu.roll(tile, far_shift, 1))
        for j in range(tiles):
            nearer = jnp.where(near_keep, near[j + 1], near[j])
            farther = jnp.where(far_keep, far[j + 1], far[j])
            send2[f][t, j] = (1.0 - weight) * nearer + weight * farther

    for f in range(fluids):
        pltpu.make_async_copy(recv1[f], recv1[f], p1_recv.at[f]).wait()

        def give(step, carry, f=f):
            t = partner(step)
            rotated(f, t)
            pltpu.make_async_remote_copy(
                src_ref=send2[f].at[t],
                dst_ref=recv2[f].at[a],
                send_sem=p2_send.at[f],
                recv_sem=p2_recv.at[f],
                device_id={"az": t},
                device_id_type=MESH,
            ).start()
            return carry

        lax.fori_loop(1, n_az, give, 0)
        rotated(f, a)
        pltpu.make_async_copy(send2[f].at[a], recv2[f].at[a], p2_recv.at[f]).start()

    for f in range(fluids):
        pltpu.make_async_copy(recv2[f], recv2[f], p2_recv.at[f]).wait()
        first = k * cycles

        def outward(i, total, f=f, first=first):
            total = total + u_s[f, first + i] * recv2[f][i]
            solved[f, i] = v_s[f, first + i] * total
            return total

        zsend[f, 0] = scale[f] * lax.fori_loop(
            0, cycles, outward, jnp.zeros(plane, jnp.float32), unroll=8
        )

        def inward(n, total, f=f, first=first):
            i = cycles - 1 - n
            solved[f, i] = scale[f] * (solved[f, i] + u_s[f, first + i] * total)
            return total + v_s[f, first + i] * recv2[f][i]

        zsend[f, 1] = scale[f] * lax.fori_loop(
            0, cycles, inward, jnp.zeros(plane, jnp.float32), unroll=8
        )
        for step in range(1, n_rad):
            t = (k + step) % n_rad
            pltpu.make_async_remote_copy(
                src_ref=zsend.at[f, jnp.where(t > k, 0, 1)],
                dst_ref=zrecv[f].at[k],
                send_sem=z_send.at[f],
                recv_sem=z_recv.at[f],
                device_id={"rad": t},
                device_id_type=MESH,
            ).start()
        zrecv[f][k] = jnp.zeros(plane, jnp.float32)

    for f in range(fluids):
        first = k * cycles
        part = zrecv[f].at[pl.ds(0, n_rad - 1)]
        pltpu.make_async_copy(part, part, z_recv.at[f]).wait()
        inner = jnp.zeros(plane, jnp.float32)
        outer = jnp.zeros(plane, jnp.float32)
        for block in range(n_rad):
            arrived = zrecv[f][block]
            inner = inner + jnp.where(block < k, arrived, 0.0)
            outer = outer + jnp.where(block > k, arrived, 0.0)

        def finish(i, carry, f=f, first=first, inner=inner, outer=outer):
            solved[f, i] = solved[f, i] + v_s[f, first + i] * inner + u_s[f, first + i] * outer
            return carry

        lax.fori_loop(0, cycles, finish, 0, unroll=8)
        pltpu.make_async_copy(solved.at[f], out.at[f], o_sem.at[f]).start()

    for f in range(fluids):
        pltpu.make_async_copy(solved.at[f], out.at[f], o_sem.at[f]).wait()
        part = recv1[f].at[pl.ds(0, n_az - 1)]
        pltpu.make_async_copy(part, part, p1_send.at[f]).wait()
        pltpu.make_async_copy(part, part, p2_send.at[f]).wait()
        part = zrecv[f].at[pl.ds(0, n_rad - 1)]
        pltpu.make_async_copy(part, part, z_send.at[f]).wait()


def per_device(grid, fields, cycle_blocks, cycle_cells, cycle_fracs, coupling):
    n_az, n_rad = lax.axis_size("az"), lax.axis_size("rad")
    fluids, cycles, vertical, width = fields.shape
    tiles = width // LANES
    plane = (tiles, vertical, LANES)
    ring = (n_az,) + plane
    tiled = fields.reshape(fluids, cycles, vertical, tiles, LANES).transpose(0, 1, 3, 2, 4)
    smem = pl.BlockSpec(memory_space=pltpu.SMEM)
    evolved = pl.pallas_call(
        functools.partial(kernel, n_az, n_rad, grid),
        out_shape=jax.ShapeDtypeStruct(tiled.shape, jnp.float32),
        in_specs=[
            pl.BlockSpec(memory_space=pl.ANY),
            smem,
            smem,
            smem,
            pl.BlockSpec(memory_space=pltpu.VMEM),
        ],
        out_specs=pl.BlockSpec(memory_space=pl.ANY),
        scratch_shapes=[pltpu.VMEM(ring, jnp.float32)] * 6
        + [
            pltpu.VMEM(tiled.shape, jnp.float32),
            pltpu.VMEM((n_rad,) + coupling.shape, jnp.float32),
            pltpu.VMEM((n_rad,) + coupling.shape, jnp.float32),
            pltpu.SMEM((n_rad,) + coupling.shape, jnp.float32),
            pltpu.SMEM((fluids, n_rad * cycles), jnp.float32),
            pltpu.SMEM((fluids, n_rad * cycles), jnp.float32),
            pltpu.VMEM((fluids, 2) + plane, jnp.float32),
            pltpu.VMEM((n_rad,) + plane, jnp.float32),
            pltpu.VMEM((n_rad,) + plane, jnp.float32),
            pltpu.SemaphoreType.DMA((fluids,)),
            pltpu.SemaphoreType.DMA((fluids,)),
            pltpu.SemaphoreType.DMA((fluids,)),
            pltpu.SemaphoreType.DMA((fluids,)),
            pltpu.SemaphoreType.DMA((fluids,)),
            pltpu.SemaphoreType.DMA((fluids,)),
            pltpu.SemaphoreType.DMA,
            pltpu.SemaphoreType.DMA,
            pltpu.SemaphoreType.DMA,
            pltpu.SemaphoreType.DMA((fluids,)),
        ],
        compiler_params=pltpu.CompilerParams(
            collective_id=0, has_side_effects=True, vmem_limit_bytes=32 * 1024 * 1024
        ),
    )(tiled, cycle_blocks.reshape(cycles), cycle_cells, cycle_fracs, coupling)
    return evolved.transpose(0, 1, 3, 2, 4).reshape(fields.shape)


def solution(mesh):
    n_az = mesh.shape["az"]
    grid = (4, 4, 2) if n_az == 32 else (1, n_az // 2, 2)
    return jax.shard_map(
        functools.partial(per_device, grid),
        mesh=mesh,
        in_specs=(P(None, "rad", None, "az"), P("rad", None), P("rad"), P("rad"), P(None, "rad")),
        out_specs=P(None, "rad", None, "az"),
        check_vma=False,
    )
```

```python
import functools

import jax
import jax.numpy as jnp
from jax import lax
from jax.experimental import pallas as pl
from jax.experimental.pallas import tpu as pltpu
from jax.sharding import PartitionSpec as P

MESH = pl.DeviceIdType.MESH
LANES = 128
PIECES = ((0, 0, 4), (1, 0, 2), (1, 2, 2))


def arrived(part, sem):
    pltpu.make_async_copy(part, part, sem).wait()


def kernel(
    n_az,
    n_rad,
    fields,
    blocks_in,
    cells_in,
    fracs_in,
    coupling,
    out,
    recv1_0,
    recv1_1,
    send2_0,
    send2_1,
    recv2_0,
    recv2_1,
    coup_all,
    rcoup,
    rcoup_s,
    u_s,
    v_s,
    blocks,
    cells,
    fracs,
    p1_send,
    p1_recv,
    p2_send,
    p2_recv,
    z_send,
    z_recv,
    c_send,
    c_recv,
    a_sem,
    *z_buffers,
):
    recv1 = (recv1_0, recv1_1)
    send2 = (send2_0, send2_1)
    recv2 = (recv2_0, recv2_1)
    zsend, zrecv = z_buffers[: len(PIECES)], z_buffers[len(PIECES) :]
    fluids, cycles, tiles, vertical, _ = fields.shape
    width = tiles * LANES
    chips = n_az // 2
    side = 4
    a = lax.axis_index("az")
    k = lax.axis_index("rad")
    chip, core = a // 2, a % 2

    def far_first(i):
        return (2 + 3 * i + 3 * (i * (i - 1) // 2)) % side

    def other_chip(step):
        x = (chip // side + far_first(step // side)) % side
        y = (chip + far_first(step % side)) % side
        return x * side + y

    barrier = pltpu.get_barrier_semaphore()
    small = [
        pltpu.make_async_copy(coupling, coup_all.at[k], a_sem.at[0]),
        pltpu.make_async_copy(blocks_in, blocks, a_sem.at[1]),
        pltpu.make_async_copy(cells_in, cells, a_sem.at[2]),
        pltpu.make_async_copy(fracs_in, fracs, a_sem.at[3]),
    ]
    for copy in small:
        copy.start()
    for step in range(1, n_rad):
        pl.semaphore_signal(barrier, inc=1, device_id={"rad": (k + step) % n_rad}, device_id_type=MESH)

    def greet(step, carry):
        t = other_chip(step)
        for c in range(2):
            pl.semaphore_signal(barrier, inc=1, device_id={"az": 2 * t + c}, device_id_type=MESH)
        return carry

    lax.fori_loop(0, chips - 1, greet, 0)
    pl.semaphore_signal(barrier, inc=1, device_id={"az": 2 * chip + 1 - core}, device_id_type=MESH)
    for copy in small:
        copy.wait()
    pl.semaphore_wait(barrier, n_az - 1 + n_rad - 1)

    for f in range(fluids):

        def send_cycle(t, f=f):
            pltpu.make_async_remote_copy(
                src_ref=fields.at[f, t],
                dst_ref=recv1[f].at[a],
                send_sem=p1_send.at[f],
                recv_sem=p1_recv.at[f],
                device_id={"az": t},
                device_id_type=MESH,
            ).start()

        def spread(step, carry, send_cycle=send_cycle):
            t = other_chip(step)
            send_cycle(2 * t)
            send_cycle(2 * t + 1)
            return carry

        lax.fori_loop(0, chips - 1, spread, 0)
        send_cycle(2 * chip + 1 - core)
        pltpu.make_async_copy(fields.at[f, a], recv1[f].at[a], p1_recv.at[f]).start()
        if f == 0:
            for step in range(1, n_rad):
                pltpu.make_async_remote_copy(
                    src_ref=coup_all.at[k],
                    dst_ref=coup_all.at[k],
                    send_sem=c_send,
                    recv_sem=c_recv,
                    device_id={"rad": (k + step) % n_rad},
                    device_id_type=MESH,
                ).start()

    arrived(coup_all.at[pl.ds(0, n_rad - 1)], c_recv)
    arrived(coup_all.at[pl.ds(0, n_rad - 1)], c_send)
    rcoup[...] = 1.0 / coup_all[...]
    to_scalar = pltpu.make_async_copy(rcoup, rcoup_s, a_sem.at[0])
    to_scalar.start()
    to_scalar.wait()

    def chain(block, carry):
        carry = list(carry)
        back = n_rad - 1 - block
        for i in range(cycles):
            j = cycles - 1 - i
            for f in range(fluids):
                u, flux, v, gain = carry[4 * f : 4 * f + 4]
                flux = flux + u
                u = u + flux * rcoup_s[block, f, i]
                u_s[f, block * cycles + i] = u
                v_s[f, back * cycles + j] = v
                gain = gain + v
                v = v + gain * rcoup_s[back, f, j]
                carry[4 * f : 4 * f + 4] = [u, flux, v, gain]
        return tuple(carry)

    one, zero = jnp.float32(1.0), jnp.float32(0.0)
    last = lax.fori_loop(0, n_rad, chain, (one, -one, one, zero) * fluids)
    tile = (vertical, LANES)
    scale = [1.0 / jnp.full(tile, last[4 * f] + last[4 * f + 1], jnp.float32) for f in range(fluids)]

    offset = width * blocks[a] + cells[a]
    shift = offset % LANES
    base = 2 * tiles * n_az - offset // LANES
    weight = fracs[a]
    lane = lax.broadcasted_iota(jnp.int32, tile, 1)
    near_keep = lane >= shift
    far_keep = lane >= shift + 1
    far_shift = (shift + 1) % LANES

    def rotated(f, t, start, count):
        near, far = [], []
        for j in range(start - 1, start + count):
            n = (base + tiles * t + j) % (tiles * n_az)
            source = recv1[f][n // tiles, n % tiles]
            near.append(pltpu.roll(source, shift, 1))
            far.append(pltpu.roll(source, far_shift, 1))
        for j in range(count):
            nearer = jnp.where(near_keep, near[j + 1], near[j])
            farther = jnp.where(far_keep, far[j + 1], far[j])
            place = start + j
            send2[f][t + place // tiles, place % tiles] = (1.0 - weight) * nearer + weight * farther

    def rotated_chip(f, t, start, count):
        if count == tiles:
            rotated(f, 2 * t, 0, 2 * tiles)
        else:
            rotated(f, 2 * t, start, count)
            rotated(f, 2 * t + 1, start, count)

    for p, (f, start, count) in enumerate(PIECES):
        if start == 0:
            arrived(recv1[f], p1_recv.at[f])

        def send_back(t, p=p, f=f, start=start, count=count):
            pltpu.make_async_remote_copy(
                src_ref=send2[f].at[t, pl.ds(start, count)],
                dst_ref=recv2[f].at[a, pl.ds(start, count)],
                send_sem=p2_send.at[p],
                recv_sem=p2_recv.at[p],
                device_id={"az": t},
                device_id_type=MESH,
            ).start()

        def give(step, carry, f=f, start=start, count=count, send_back=send_back):
            t = other_chip(step)
            rotated_chip(f, t, start, count)
            send_back(2 * t)
            send_back(2 * t + 1)
            return carry

        lax.fori_loop(0, chips - 1, give, 0)
        rotated_chip(f, chip, start, count)
        send_back(2 * chip + 1 - core)
        part = pl.ds(start, count)
        pltpu.make_async_copy(send2[f].at[a, part], recv2[f].at[a, part], p2_recv.at[p]).start()

    first = k * cycles

    def solve(p):
        f, start, count = PIECES[p]
        part = pl.ds(start, count)
        plane = (count, vertical, LANES)
        arrived(recv2[f].at[pl.ds(0, n_az), part], p2_recv.at[p])

        def outward(i, total):
            total = total + u_s[f, first + i] * recv2[f][i, part]
            out[f, i, part] = v_s[f, first + i] * total
            return total

        zsend[p][0] = scale[f] * lax.fori_loop(0, cycles, outward, jnp.zeros(plane, jnp.float32), unroll=8)

        def inward(n, total):
            i = cycles - 1 - n
            out[f, i, part] = scale[f] * (out[f, i, part] + u_s[f, first + i] * total)
            return total + v_s[f, first + i] * recv2[f][i, part]

        zsend[p][1] = scale[f] * lax.fori_loop(0, cycles, inward, jnp.zeros(plane, jnp.float32), unroll=8)
        for step in range(1, n_rad):
            t = (k + step) % n_rad
            pltpu.make_async_remote_copy(
                src_ref=zsend[p].at[jnp.where(t > k, 0, 1)],
                dst_ref=zrecv[p].at[k],
                send_sem=z_send.at[p],
                recv_sem=z_recv.at[p],
                device_id={"rad": t},
                device_id_type=MESH,
            ).start()
        zrecv[p][k] = jnp.zeros(plane, jnp.float32)

    def finish(p):
        f, start, count = PIECES[p]
        part = pl.ds(start, count)
        arrived(zrecv[p].at[pl.ds(0, n_rad - 1)], z_recv.at[p])
        inner = jnp.zeros((count, vertical, LANES), jnp.float32)
        outer = inner
        for block in range(n_rad):
            sums = zrecv[p][block]
            inner = inner + jnp.where(block < k, sums, 0.0)
            outer = outer + jnp.where(block > k, sums, 0.0)

        def add(i, carry):
            out[f, i, part] = out[f, i, part] + v_s[f, first + i] * inner + u_s[f, first + i] * outer
            return carry

        lax.fori_loop(0, cycles, add, 0, unroll=8)

    for p in range(len(PIECES)):
        solve(p)
        if p > 0:
            finish(p - 1)
    finish(len(PIECES) - 1)

    for f in range(fluids):
        arrived(recv1[f].at[pl.ds(0, n_az - 1)], p1_send.at[f])
    for p, (f, start, count) in enumerate(PIECES):
        arrived(recv2[f].at[pl.ds(0, n_az - 1), pl.ds(start, count)], p2_send.at[p])
        arrived(zrecv[p].at[pl.ds(0, n_rad - 1)], z_send.at[p])


def per_device(fields, cycle_blocks, cycle_cells, cycle_fracs, coupling):
    n_az, n_rad = lax.axis_size("az"), lax.axis_size("rad")
    fluids, cycles, vertical, width = fields.shape
    tiles = width // LANES
    ring = pltpu.VMEM((n_az, tiles, vertical, LANES), jnp.float32)
    pieces = len(PIECES)
    tiled = fields.reshape(fluids, cycles, vertical, tiles, LANES).transpose(0, 1, 3, 2, 4)
    operands = [tiled, cycle_blocks.reshape(cycles), cycle_cells, cycle_fracs, coupling]
    operands = [pltpu.with_memory_space_constraint(x, pltpu.HBM) for x in operands]
    every = (n_rad, fluids, cycles)
    evolved = pl.pallas_call(
        functools.partial(kernel, n_az, n_rad),
        out_shape=pltpu.VMEM(tiled.shape, jnp.float32),
        in_specs=[pl.BlockSpec(memory_space=pltpu.HBM)] * 5,
        out_specs=pl.BlockSpec(memory_space=pltpu.VMEM),
        scratch_shapes=[ring] * 6
        + [
            pltpu.VMEM(every, jnp.float32),
            pltpu.VMEM(every, jnp.float32),
            pltpu.SMEM(every, jnp.float32),
            pltpu.SMEM((fluids, n_rad * cycles), jnp.float32),
            pltpu.SMEM((fluids, n_rad * cycles), jnp.float32),
            pltpu.SMEM((cycles,), jnp.int32),
            pltpu.SMEM((cycles,), jnp.int32),
            pltpu.SMEM((cycles,), jnp.float32),
            pltpu.SemaphoreType.DMA((fluids,)),
            pltpu.SemaphoreType.DMA((fluids,)),
            pltpu.SemaphoreType.DMA((pieces,)),
            pltpu.SemaphoreType.DMA((pieces,)),
            pltpu.SemaphoreType.DMA((pieces,)),
            pltpu.SemaphoreType.DMA((pieces,)),
            pltpu.SemaphoreType.DMA,
            pltpu.SemaphoreType.DMA,
            pltpu.SemaphoreType.DMA((4,)),
        ]
        + [pltpu.VMEM((2, count, vertical, LANES), jnp.float32) for _, _, count in PIECES]
        + [pltpu.VMEM((n_rad, count, vertical, LANES), jnp.float32) for _, _, count in PIECES],
        compiler_params=pltpu.CompilerParams(
            collective_id=0, has_side_effects=True, vmem_limit_bytes=32 * 1024 * 1024
        ),
    )(*operands)
    return evolved.transpose(0, 1, 3, 2, 4).reshape(fields.shape)


def solution(mesh):
    return jax.shard_map(
        per_device,
        mesh=mesh,
        in_specs=(P(None, "rad", None, "az"), P("rad", None), P("rad"), P("rad"), P(None, "rad")),
        out_specs=P(None, "rad", None, "az"),
        check_vma=False,
    )
```

```python
import functools

import jax
import jax.numpy as jnp
from jax import lax
from jax.experimental import pallas as pl
from jax.experimental.pallas import tpu as pltpu
from jax.sharding import PartitionSpec as P

MESH = pl.DeviceIdType.MESH
LANES = 128
PIECES = ((0, 0, 2), (0, 2, 2), (1, 0, 2), (1, 2, 2))
AHEAD = 3


def arrived(part, sem):
    pltpu.make_async_copy(part, part, sem).wait()


def kernel(
    n_az,
    n_rad,
    fields,
    blocks_in,
    cells_in,
    fracs_in,
    coupling,
    out,
    recv1_0,
    recv1_1,
    send2_0,
    send2_1,
    recv2_0,
    recv2_1,
    coup_all,
    rcoup,
    rcoup_s,
    u_s,
    v_s,
    blocks,
    cells,
    fracs,
    p1_send,
    p1_recv,
    p2_send,
    p2_recv,
    z_send,
    z_recv,
    c_send,
    c_recv,
    a_sem,
    *z_buffers,
):
    recv1 = (recv1_0, recv1_1)
    send2 = (send2_0, send2_1)
    recv2 = (recv2_0, recv2_1)
    zsend, zrecv = z_buffers[: len(PIECES)], z_buffers[len(PIECES) :]
    fluids, cycles, tiles, vertical, _ = fields.shape
    width = tiles * LANES
    chips = n_az // 2
    side = 4
    a = lax.axis_index("az")
    k = lax.axis_index("rad")
    chip, core = a >> 1, a & 1

    def far_first(i):
        return 2 + 3 * i + 3 * (i * (i - 1) >> 1)

    def other_chip(step):
        x = ((chip >> 2) + far_first(step >> 2)) & (side - 1)
        y = (chip + far_first(step & (side - 1))) & (side - 1)
        return x * side + y

    barrier = pltpu.get_barrier_semaphore()
    small = [
        pltpu.make_async_copy(coupling, coup_all.at[k], a_sem.at[0]),
        pltpu.make_async_copy(blocks_in, blocks, a_sem.at[1]),
        pltpu.make_async_copy(cells_in, cells, a_sem.at[2]),
        pltpu.make_async_copy(fracs_in, fracs, a_sem.at[3]),
    ]
    for copy in small:
        copy.start()
    for step in range(1, n_rad):
        pl.semaphore_signal(barrier, inc=1, device_id={"rad": (k + step) % n_rad}, device_id_type=MESH)

    def greet(step, carry):
        t = other_chip(step)
        for c in range(2):
            pl.semaphore_signal(barrier, inc=1, device_id={"az": 2 * t + c}, device_id_type=MESH)
        return carry

    lax.fori_loop(0, chips - 1, greet, 0)
    pl.semaphore_signal(barrier, inc=1, device_id={"az": 2 * chip + 1 - core}, device_id_type=MESH)
    pl.semaphore_wait(barrier, n_az - 1 + n_rad - 1)

    for f in range(fluids):

        def send_cycle(t, f=f):
            pltpu.make_async_remote_copy(
                src_ref=fields.at[f, t],
                dst_ref=recv1[f].at[pl.ds(tiles * a, tiles)],
                send_sem=p1_send.at[f],
                recv_sem=p1_recv.at[f],
                device_id={"az": t},
                device_id_type=MESH,
            ).start()

        def spread(step, carry, send_cycle=send_cycle):
            t = other_chip(step)
            send_cycle(2 * t)
            send_cycle(2 * t + 1)
            return carry

        lax.fori_loop(0, chips - 1, spread, 0)
        send_cycle(2 * chip + 1 - core)
        pltpu.make_async_copy(fields.at[f, a], recv1[f].at[pl.ds(tiles * a, tiles)], p1_recv.at[f]).start()
        if f == 0:
            for copy in small:
                copy.wait()
            for step in range(1, n_rad):
                pltpu.make_async_remote_copy(
                    src_ref=coup_all.at[k],
                    dst_ref=coup_all.at[k],
                    send_sem=c_send,
                    recv_sem=c_recv,
                    device_id={"rad": (k + step) % n_rad},
                    device_id_type=MESH,
                ).start()

    arrived(coup_all.at[pl.ds(0, n_rad - 1)], c_recv)
    arrived(coup_all.at[pl.ds(0, n_rad - 1)], c_send)
    rcoup[...] = 1.0 / coup_all[...]
    to_scalar = pltpu.make_async_copy(rcoup, rcoup_s, a_sem.at[0])
    to_scalar.start()
    to_scalar.wait()

    def chain(block, carry):
        carry = list(carry)
        back = n_rad - 1 - block
        for i in range(cycles):
            j = cycles - 1 - i
            for f in range(fluids):
                u, flux, v, gain = carry[4 * f : 4 * f + 4]
                flux = flux + u
                u = u + flux * rcoup_s[block, f, i]
                u_s[f, block * cycles + i] = u
                v_s[f, back * cycles + j] = v
                gain = gain + v
                v = v + gain * rcoup_s[back, f, j]
                carry[4 * f : 4 * f + 4] = [u, flux, v, gain]
        return tuple(carry)

    one, zero = jnp.float32(1.0), jnp.float32(0.0)
    last = lax.fori_loop(0, n_rad, chain, (one, -one, one, zero) * fluids)
    tile = (vertical, LANES)
    scale = [1.0 / jnp.full(tile, last[4 * f] + last[4 * f + 1], jnp.float32) for f in range(fluids)]

    offset = width * blocks[a] + cells[a]
    shift = offset % LANES
    base = 2 * tiles * n_az - offset // LANES
    weight = fracs[a]
    lane = lax.broadcasted_iota(jnp.int32, tile, 1)
    near_keep = lane >= shift
    far_keep = lane >= shift + 1
    far_shift = (shift + 1) % LANES

    def rotated_chip(f, t):
        near, far = [], []
        for j in range(-1, 2 * tiles):
            source = recv1[f][(base + (2 * tiles * t + j)) & (tiles * n_az - 1)]
            near.append(pltpu.roll(source, shift, 1))
            far.append(pltpu.roll(source, far_shift, 1))
        for j in range(2 * tiles):
            nearer = jnp.where(near_keep, near[j + 1], near[j])
            farther = jnp.where(far_keep, far[j + 1], far[j])
            send2[f][2 * t + j // tiles, j % tiles] = (1.0 - weight) * nearer + weight * farther

    def go_back(p):
        f, start, count = PIECES[p]
        part = pl.ds(start, count)
        if start == 0:
            arrived(recv1[f], p1_recv.at[f])

        def send_back(t):
            pltpu.make_async_remote_copy(
                src_ref=send2[f].at[t, part],
                dst_ref=recv2[f].at[a, part],
                send_sem=p2_send.at[p],
                recv_sem=p2_recv.at[p],
                device_id={"az": t},
                device_id_type=MESH,
            ).start()

        def give(step, carry):
            t = other_chip(step)
            if start == 0:
                rotated_chip(f, t)
            send_back(2 * t)
            send_back(2 * t + 1)
            return carry

        lax.fori_loop(0, chips - 1, give, 0)
        if start == 0:
            rotated_chip(f, chip)
        send_back(2 * chip + 1 - core)
        pltpu.make_async_copy(send2[f].at[a, part], recv2[f].at[a, part], p2_recv.at[p]).start()

    first = k * cycles

    def share(p):
        f, start, count = PIECES[p]
        part = pl.ds(start, count)
        plane = (count, vertical, LANES)
        arrived(recv2[f].at[pl.ds(0, n_az), part], p2_recv.at[p])
        nothing = jnp.zeros(plane, jnp.float32)

        def add(n, sums):
            sums = list(sums)
            for j in range(8):
                i = 8 * n + j
                row = recv2[f][i, part]
                sums[j % 2] += u_s[f, first + i] * row
                sums[2 + j % 2] += v_s[f, first + i] * row
            return tuple(sums)

        sums = lax.fori_loop(0, cycles // 8, add, (nothing,) * 4, unroll=True)
        zsend[p][0] = scale[f] * (sums[0] + sums[1])
        zsend[p][1] = scale[f] * (sums[2] + sums[3])
        for step in range(1, n_rad):
            t = (k + step) % n_rad
            pltpu.make_async_remote_copy(
                src_ref=zsend[p].at[jnp.where(t > k, 0, 1)],
                dst_ref=zrecv[p].at[k],
                send_sem=z_send.at[p],
                recv_sem=z_recv.at[p],
                device_id={"rad": t},
                device_id_type=MESH,
            ).start()
        zrecv[p][k] = nothing

    def solve(p):
        f, start, count = PIECES[p]
        part = pl.ds(start, count)
        nothing = jnp.zeros((count, vertical, LANES), jnp.float32)

        def outward(i, total):
            total = total + u_s[f, first + i] * recv2[f][i, part]
            out[f, i, part] = v_s[f, first + i] * total
            return total

        lax.fori_loop(0, cycles, outward, nothing, unroll=8)

        def inward(n, total):
            i = cycles - 1 - n
            out[f, i, part] = scale[f] * (out[f, i, part] + u_s[f, first + i] * total)
            return total + v_s[f, first + i] * recv2[f][i, part]

        lax.fori_loop(0, cycles, inward, nothing, unroll=8)

    def finish(p):
        f, start, count = PIECES[p]
        part = pl.ds(start, count)
        arrived(zrecv[p].at[pl.ds(0, n_rad - 1)], z_recv.at[p])
        inner = jnp.zeros((count, vertical, LANES), jnp.float32)
        outer = inner
        for block in range(n_rad):
            sums = zrecv[p][block]
            inner = inner + jnp.where(block < k, sums, 0.0)
            outer = outer + jnp.where(block > k, sums, 0.0)

        def add(i, carry):
            out[f, i, part] = out[f, i, part] + v_s[f, first + i] * inner + u_s[f, first + i] * outer
            return carry

        lax.fori_loop(0, cycles, add, 0, unroll=8)

    for p in range(len(PIECES)):
        if p >= AHEAD:
            share(p - AHEAD)
        go_back(p)
        if p >= AHEAD:
            solve(p - AHEAD)
            if p > AHEAD:
                finish(p - AHEAD - 1)
    for p in range(len(PIECES) - AHEAD, len(PIECES)):
        share(p)
        solve(p)
        if p > 0:
            finish(p - 1)
    finish(len(PIECES) - 1)

    for f in range(fluids):
        arrived(recv1[f].at[pl.ds(0, tiles * (n_az - 1))], p1_send.at[f])
    for p, (f, start, count) in enumerate(PIECES):
        arrived(recv2[f].at[pl.ds(0, n_az - 1), pl.ds(start, count)], p2_send.at[p])
        arrived(zrecv[p].at[pl.ds(0, n_rad - 1)], z_send.at[p])


def per_device(fields, cycle_blocks, cycle_cells, cycle_fracs, coupling):
    n_az, n_rad = lax.axis_size("az"), lax.axis_size("rad")
    fluids, cycles, vertical, width = fields.shape
    tiles = width // LANES
    ring = pltpu.VMEM((n_az, tiles, vertical, LANES), jnp.float32)
    flat = pltpu.VMEM((n_az * tiles, vertical, LANES), jnp.float32)
    pieces = len(PIECES)
    tiled = fields.reshape(fluids, cycles, vertical, tiles, LANES).transpose(0, 1, 3, 2, 4)
    operands = [tiled, cycle_blocks.reshape(cycles), cycle_cells, cycle_fracs, coupling]
    operands = [pltpu.with_memory_space_constraint(x, pltpu.HBM) for x in operands]
    every = (n_rad, fluids, cycles)
    evolved = pl.pallas_call(
        functools.partial(kernel, n_az, n_rad),
        out_shape=pltpu.VMEM(tiled.shape, jnp.float32),
        in_specs=[pl.BlockSpec(memory_space=pltpu.HBM)] * 5,
        out_specs=pl.BlockSpec(memory_space=pltpu.VMEM),
        scratch_shapes=[flat] * 2 + [ring] * 4
        + [
            pltpu.VMEM(every, jnp.float32),
            pltpu.VMEM(every, jnp.float32),
            pltpu.SMEM(every, jnp.float32),
            pltpu.SMEM((fluids, n_rad * cycles), jnp.float32),
            pltpu.SMEM((fluids, n_rad * cycles), jnp.float32),
            pltpu.SMEM((cycles,), jnp.int32),
            pltpu.SMEM((cycles,), jnp.int32),
            pltpu.SMEM((cycles,), jnp.float32),
            pltpu.SemaphoreType.DMA((fluids,)),
            pltpu.SemaphoreType.DMA((fluids,)),
            pltpu.SemaphoreType.DMA((pieces,)),
            pltpu.SemaphoreType.DMA((pieces,)),
            pltpu.SemaphoreType.DMA((pieces,)),
            pltpu.SemaphoreType.DMA((pieces,)),
            pltpu.SemaphoreType.DMA,
            pltpu.SemaphoreType.DMA,
            pltpu.SemaphoreType.DMA((4,)),
        ]
        + [pltpu.VMEM((2, count, vertical, LANES), jnp.float32) for _, _, count in PIECES]
        + [pltpu.VMEM((n_rad, count, vertical, LANES), jnp.float32) for _, _, count in PIECES],
        compiler_params=pltpu.CompilerParams(
            collective_id=0, has_side_effects=True, vmem_limit_bytes=32 * 1024 * 1024
        ),
    )(*operands)
    return evolved.transpose(0, 1, 3, 2, 4).reshape(fields.shape)


def solution(mesh):
    return jax.shard_map(
        per_device,
        mesh=mesh,
        in_specs=(P(None, "rad", None, "az"), P("rad", None), P("rad"), P("rad"), P(None, "rad")),
        out_specs=P(None, "rad", None, "az"),
        check_vma=False,
    )
```

```python
import functools

import jax
import jax.numpy as jnp
from jax import lax
from jax.experimental import pallas as pl
from jax.experimental.pallas import tpu as pltpu
from jax.sharding import PartitionSpec as P

MESH = pl.DeviceIdType.MESH
LANES = 128
PIECES = ((0, 0, 2), (0, 2, 2), (1, 0, 2), (1, 2, 2))
AHEAD = 3


def arrived(part, sem):
    pltpu.make_async_copy(part, part, sem).wait()


def kernel(
    n_az,
    n_rad,
    fields,
    blocks_in,
    cells_in,
    fracs_in,
    coupling,
    out,
    recv1_0,
    recv1_1,
    send2_0,
    send2_1,
    recv2_0,
    recv2_1,
    coup_all,
    rcoup,
    rcoup_s,
    u_s,
    v_s,
    blocks,
    cells,
    fracs,
    p1_send,
    p1_recv,
    p2_send,
    p2_recv,
    z_send,
    z_recv,
    c_send,
    c_recv,
    a_sem,
    *z_buffers,
):
    recv1 = (recv1_0, recv1_1)
    send2 = (send2_0, send2_1)
    recv2 = (recv2_0, recv2_1)
    zsend, zrecv = z_buffers[: len(PIECES)], z_buffers[len(PIECES) :]
    fluids, cycles, tiles, vertical, _ = fields.shape
    width = tiles * LANES
    chips = n_az // 2
    side = 4
    a = lax.axis_index("az")
    k = lax.axis_index("rad")
    chip, core = a >> 1, a & 1

    def far_first(i):
        return 2 + 3 * i + 3 * (i * (i - 1) >> 1)

    def other_chip(step):
        turn = 1 - 2 * core
        x = ((chip >> 2) + turn * far_first(step >> 2)) & (side - 1)
        y = (chip + turn * far_first(step & (side - 1))) & (side - 1)
        return x * side + y

    barrier = pltpu.get_barrier_semaphore()
    small = [
        pltpu.make_async_copy(coupling, coup_all.at[k], a_sem.at[0]),
        pltpu.make_async_copy(blocks_in, blocks, a_sem.at[1]),
        pltpu.make_async_copy(cells_in, cells, a_sem.at[2]),
        pltpu.make_async_copy(fracs_in, fracs, a_sem.at[3]),
    ]
    for copy in small:
        copy.start()
    for step in range(1, n_rad):
        pl.semaphore_signal(barrier, inc=1, device_id={"rad": (k + step) % n_rad}, device_id_type=MESH)

    def greet(step, carry):
        t = other_chip(step)
        for c in range(2):
            pl.semaphore_signal(barrier, inc=1, device_id={"az": 2 * t + c}, device_id_type=MESH)
        return carry

    lax.fori_loop(0, chips - 1, greet, 0)
    pl.semaphore_signal(barrier, inc=1, device_id={"az": 2 * chip + 1 - core}, device_id_type=MESH)
    pl.semaphore_wait(barrier, n_az - 1 + n_rad - 1)

    for f in range(fluids):

        def send_cycle(t, f=f):
            pltpu.make_async_remote_copy(
                src_ref=fields.at[f, t],
                dst_ref=recv1[f].at[pl.ds(tiles * a, tiles)],
                send_sem=p1_send.at[f],
                recv_sem=p1_recv.at[f],
                device_id={"az": t},
                device_id_type=MESH,
            ).start()

        def spread(step, carry, send_cycle=send_cycle):
            t = other_chip(step)
            send_cycle(2 * t + core)
            send_cycle(2 * t + 1 - core)
            return carry

        lax.fori_loop(0, chips - 1, spread, 0)
        send_cycle(2 * chip + 1 - core)
        pltpu.make_async_copy(fields.at[f, a], recv1[f].at[pl.ds(tiles * a, tiles)], p1_recv.at[f]).start()
        if f == 0:
            for copy in small:
                copy.wait()
            for step in range(1, n_rad):
                pltpu.make_async_remote_copy(
                    src_ref=coup_all.at[k],
                    dst_ref=coup_all.at[k],
                    send_sem=c_send,
                    recv_sem=c_recv,
                    device_id={"rad": (k + step) % n_rad},
                    device_id_type=MESH,
                ).start()

    arrived(coup_all.at[pl.ds(0, n_rad - 1)], c_recv)
    arrived(coup_all.at[pl.ds(0, n_rad - 1)], c_send)
    rcoup[...] = 1.0 / coup_all[...]
    to_scalar = pltpu.make_async_copy(rcoup, rcoup_s, a_sem.at[0])
    to_scalar.start()
    to_scalar.wait()

    def chain(block, carry):
        carry = list(carry)
        back = n_rad - 1 - block
        for i in range(cycles):
            j = cycles - 1 - i
            for f in range(fluids):
                u, flux, v, gain = carry[4 * f : 4 * f + 4]
                flux = flux + u
                u = u + flux * rcoup_s[block, f, i]
                u_s[f, block * cycles + i] = u
                v_s[f, back * cycles + j] = v
                gain = gain + v
                v = v + gain * rcoup_s[back, f, j]
                carry[4 * f : 4 * f + 4] = [u, flux, v, gain]
        return tuple(carry)

    one, zero = jnp.float32(1.0), jnp.float32(0.0)
    last = lax.fori_loop(0, n_rad, chain, (one, -one, one, zero) * fluids)
    tile = (vertical, LANES)
    scale = [1.0 / jnp.full(tile, last[4 * f] + last[4 * f + 1], jnp.float32) for f in range(fluids)]

    offset = width * blocks[a] + cells[a]
    shift = offset % LANES
    base = 2 * tiles * n_az - offset // LANES
    weight = fracs[a]
    lane = lax.broadcasted_iota(jnp.int32, tile, 1)
    near_keep = lane >= shift
    far_keep = lane >= shift + 1
    far_shift = (shift + 1) % LANES

    def rotated_chip(f, t):
        near, far = [], []
        for j in range(-1, 2 * tiles):
            source = recv1[f][(base + (2 * tiles * t + j)) & (tiles * n_az - 1)]
            near.append(pltpu.roll(source, shift, 1))
            far.append(pltpu.roll(source, far_shift, 1))
        for j in range(2 * tiles):
            nearer = jnp.where(near_keep, near[j + 1], near[j])
            farther = jnp.where(far_keep, far[j + 1], far[j])
            send2[f][2 * t + j // tiles, j % tiles] = (1.0 - weight) * nearer + weight * farther

    def go_back(p):
        f, start, count = PIECES[p]
        part = pl.ds(start, count)
        if start == 0:
            arrived(recv1[f], p1_recv.at[f])

        def send_back(t):
            pltpu.make_async_remote_copy(
                src_ref=send2[f].at[t, part],
                dst_ref=recv2[f].at[a, part],
                send_sem=p2_send.at[p],
                recv_sem=p2_recv.at[p],
                device_id={"az": t},
                device_id_type=MESH,
            ).start()

        def give(step, carry):
            t = other_chip(step)
            if start == 0:
                rotated_chip(f, t)
            send_back(2 * t + core)
            send_back(2 * t + 1 - core)
            return carry

        lax.fori_loop(0, chips - 1, give, 0)
        if start == 0:
            rotated_chip(f, chip)
        send_back(2 * chip + 1 - core)
        pltpu.make_async_copy(send2[f].at[a, part], recv2[f].at[a, part], p2_recv.at[p]).start()

    first = k * cycles

    def share(p):
        f, start, count = PIECES[p]
        part = pl.ds(start, count)
        plane = (count, vertical, LANES)
        arrived(recv2[f].at[pl.ds(0, n_az), part], p2_recv.at[p])
        nothing = jnp.zeros(plane, jnp.float32)

        def add(n, sums):
            sums = list(sums)
            for j in range(8):
                i = 8 * n + j
                row = recv2[f][i, part]
                sums[j % 2] += u_s[f, first + i] * row
                sums[2 + j % 2] += v_s[f, first + i] * row
            return tuple(sums)

        sums = lax.fori_loop(0, cycles // 8, add, (nothing,) * 4, unroll=True)
        zsend[p][0] = scale[f] * (sums[0] + sums[1])
        zsend[p][1] = scale[f] * (sums[2] + sums[3])
        for step in range(1, n_rad):
            t = (k + step) % n_rad
            pltpu.make_async_remote_copy(
                src_ref=zsend[p].at[jnp.where(t > k, 0, 1)],
                dst_ref=zrecv[p].at[k],
                send_sem=z_send.at[p],
                recv_sem=z_recv.at[p],
                device_id={"rad": t},
                device_id_type=MESH,
            ).start()
        zrecv[p][k] = nothing

    def solve(p):
        f, start, count = PIECES[p]
        part = pl.ds(start, count)
        nothing = jnp.zeros((count, vertical, LANES), jnp.float32)

        def outward(i, total):
            total = total + u_s[f, first + i] * recv2[f][i, part]
            out[f, i, part] = v_s[f, first + i] * total
            return total

        lax.fori_loop(0, cycles, outward, nothing, unroll=8)

        def inward(n, total):
            i = cycles - 1 - n
            out[f, i, part] = scale[f] * (out[f, i, part] + u_s[f, first + i] * total)
            return total + v_s[f, first + i] * recv2[f][i, part]

        lax.fori_loop(0, cycles, inward, nothing, unroll=8)

    def finish(p):
        f, start, count = PIECES[p]
        part = pl.ds(start, count)
        arrived(zrecv[p].at[pl.ds(0, n_rad - 1)], z_recv.at[p])
        inner = jnp.zeros((count, vertical, LANES), jnp.float32)
        outer = inner
        for block in range(n_rad):
            sums = zrecv[p][block]
            inner = inner + jnp.where(block < k, sums, 0.0)
            outer = outer + jnp.where(block > k, sums, 0.0)

        def add(i, carry):
            out[f, i, part] = out[f, i, part] + v_s[f, first + i] * inner + u_s[f, first + i] * outer
            return carry

        lax.fori_loop(0, cycles, add, 0, unroll=8)

    for p in range(len(PIECES)):
        if p >= AHEAD:
            share(p - AHEAD)
        go_back(p)
        if p >= AHEAD:
            solve(p - AHEAD)
            if p > AHEAD:
                finish(p - AHEAD - 1)
    for p in range(len(PIECES) - AHEAD, len(PIECES)):
        share(p)
        solve(p)
        if p > 0:
            finish(p - 1)
    finish(len(PIECES) - 1)

    for f in range(fluids):
        arrived(recv1[f].at[pl.ds(0, tiles * (n_az - 1))], p1_send.at[f])
    for p, (f, start, count) in enumerate(PIECES):
        arrived(recv2[f].at[pl.ds(0, n_az - 1), pl.ds(start, count)], p2_send.at[p])
        arrived(zrecv[p].at[pl.ds(0, n_rad - 1)], z_send.at[p])


def per_device(fields, cycle_blocks, cycle_cells, cycle_fracs, coupling):
    n_az, n_rad = lax.axis_size("az"), lax.axis_size("rad")
    fluids, cycles, vertical, width = fields.shape
    tiles = width // LANES
    ring = pltpu.VMEM((n_az, tiles, vertical, LANES), jnp.float32)
    flat = pltpu.VMEM((n_az * tiles, vertical, LANES), jnp.float32)
    pieces = len(PIECES)
    tiled = fields.reshape(fluids, cycles, vertical, tiles, LANES).transpose(0, 1, 3, 2, 4)
    operands = [tiled, cycle_blocks.reshape(cycles), cycle_cells, cycle_fracs, coupling]
    operands = [pltpu.with_memory_space_constraint(x, pltpu.HBM) for x in operands]
    every = (n_rad, fluids, cycles)
    evolved = pl.pallas_call(
        functools.partial(kernel, n_az, n_rad),
        out_shape=pltpu.VMEM(tiled.shape, jnp.float32),
        in_specs=[pl.BlockSpec(memory_space=pltpu.HBM)] * 5,
        out_specs=pl.BlockSpec(memory_space=pltpu.VMEM),
        scratch_shapes=[flat] * 2 + [ring] * 4
        + [
            pltpu.VMEM(every, jnp.float32),
            pltpu.VMEM(every, jnp.float32),
            pltpu.SMEM(every, jnp.float32),
            pltpu.SMEM((fluids, n_rad * cycles), jnp.float32),
            pltpu.SMEM((fluids, n_rad * cycles), jnp.float32),
            pltpu.SMEM((cycles,), jnp.int32),
            pltpu.SMEM((cycles,), jnp.int32),
            pltpu.SMEM((cycles,), jnp.float32),
            pltpu.SemaphoreType.DMA((fluids,)),
            pltpu.SemaphoreType.DMA((fluids,)),
            pltpu.SemaphoreType.DMA((pieces,)),
            pltpu.SemaphoreType.DMA((pieces,)),
            pltpu.SemaphoreType.DMA((pieces,)),
            pltpu.SemaphoreType.DMA((pieces,)),
            pltpu.SemaphoreType.DMA,
            pltpu.SemaphoreType.DMA,
            pltpu.SemaphoreType.DMA((4,)),
        ]
        + [pltpu.VMEM((2, count, vertical, LANES), jnp.float32) for _, _, count in PIECES]
        + [pltpu.VMEM((n_rad, count, vertical, LANES), jnp.float32) for _, _, count in PIECES],
        compiler_params=pltpu.CompilerParams(
            collective_id=0, has_side_effects=True, vmem_limit_bytes=32 * 1024 * 1024
        ),
    )(*operands)
    return evolved.transpose(0, 1, 3, 2, 4).reshape(fields.shape)


def solution(mesh):
    return jax.shard_map(
        per_device,
        mesh=mesh,
        in_specs=(P(None, "rad", None, "az"), P("rad", None), P("rad"), P("rad"), P(None, "rad")),
        out_specs=P(None, "rad", None, "az"),
        check_vma=False,
    )
```

```python
import functools

import jax
import jax.numpy as jnp
from jax import lax
from jax.experimental import pallas as pl
from jax.experimental.pallas import tpu as pltpu
from jax.sharding import PartitionSpec as P

MESH = pl.DeviceIdType.MESH
LANES = 128
PIECES = ((0, 0, 2), (0, 2, 2), (1, 0, 2), (1, 2, 2))
AHEAD = 3


def arrived(part, sem):
    pltpu.make_async_copy(part, part, sem).wait()


def kernel(
    n_az,
    n_rad,
    fields,
    blocks_in,
    cells_in,
    fracs_in,
    coupling,
    out,
    edges,
    table,
    recv1_0,
    recv1_1,
    send2_0,
    send2_1,
    recv2_0,
    recv2_1,
    coup_all,
    rcoup,
    rcoup_s,
    u_s,
    v_s,
    blocks,
    cells,
    fracs,
    p1_send,
    p1_recv,
    p2_send,
    p2_recv,
    z_send,
    z_recv,
    c_send,
    c_recv,
    a_sem,
    *z_buffers,
):
    recv1 = (recv1_0, recv1_1)
    send2 = (send2_0, send2_1)
    recv2 = (recv2_0, recv2_1)
    zsend, zrecv = z_buffers[: len(PIECES)], z_buffers[len(PIECES) :]
    fluids, cycles, tiles, vertical, _ = fields.shape
    width = tiles * LANES
    chips = n_az // 2
    side = 4
    a = lax.axis_index("az")
    k = lax.axis_index("rad")
    chip, core = a >> 1, a & 1

    def far_first(i):
        return 2 + 3 * i + 3 * (i * (i - 1) >> 1)

    def other_chip(step):
        turn = 1 - 2 * core
        x = ((chip >> 2) + turn * far_first(step >> 2)) & (side - 1)
        y = (chip + turn * far_first(step & (side - 1))) & (side - 1)
        return x * side + y

    barrier = pltpu.get_barrier_semaphore()
    small = [
        pltpu.make_async_copy(coupling, coup_all.at[k], a_sem.at[0]),
        pltpu.make_async_copy(blocks_in, blocks, a_sem.at[1]),
        pltpu.make_async_copy(cells_in, cells, a_sem.at[2]),
        pltpu.make_async_copy(fracs_in, fracs, a_sem.at[3]),
    ]
    for copy in small:
        copy.start()
    for step in range(1, n_rad):
        pl.semaphore_signal(barrier, inc=1, device_id={"rad": (k + step) % n_rad}, device_id_type=MESH)

    def greet(step, carry):
        t = other_chip(step)
        for c in range(2):
            pl.semaphore_signal(barrier, inc=1, device_id={"az": 2 * t + c}, device_id_type=MESH)
        return carry

    lax.fori_loop(0, chips - 1, greet, 0)
    pl.semaphore_signal(barrier, inc=1, device_id={"az": 2 * chip + 1 - core}, device_id_type=MESH)
    pl.semaphore_wait(barrier, n_az - 1 + n_rad - 1)

    for f in range(fluids):

        def send_cycle(t, f=f):
            pltpu.make_async_remote_copy(
                src_ref=fields.at[f, t],
                dst_ref=recv1[f].at[pl.ds(tiles * a, tiles)],
                send_sem=p1_send.at[f],
                recv_sem=p1_recv.at[f],
                device_id={"az": t},
                device_id_type=MESH,
            ).start()

        def spread(step, carry, send_cycle=send_cycle):
            t = other_chip(step)
            send_cycle(2 * t + core)
            send_cycle(2 * t + 1 - core)
            return carry

        lax.fori_loop(0, chips - 1, spread, 0)
        send_cycle(2 * chip + 1 - core)
        pltpu.make_async_copy(fields.at[f, a], recv1[f].at[pl.ds(tiles * a, tiles)], p1_recv.at[f]).start()
        if f == 0:
            for copy in small:
                copy.wait()
            for step in range(1, n_rad):
                pltpu.make_async_remote_copy(
                    src_ref=coup_all.at[k],
                    dst_ref=coup_all.at[k],
                    send_sem=c_send,
                    recv_sem=c_recv,
                    device_id={"rad": (k + step) % n_rad},
                    device_id_type=MESH,
                ).start()

    arrived(coup_all.at[pl.ds(0, n_rad - 1)], c_recv)
    arrived(coup_all.at[pl.ds(0, n_rad - 1)], c_send)
    rcoup[...] = 1.0 / coup_all[...]
    to_scalar = pltpu.make_async_copy(rcoup, rcoup_s, a_sem.at[0])
    to_scalar.start()
    to_scalar.wait()

    def chain(block, carry):
        carry = list(carry)
        back = n_rad - 1 - block
        for i in range(cycles):
            j = cycles - 1 - i
            for f in range(fluids):
                u, flux, v, gain = carry[4 * f : 4 * f + 4]
                flux = flux + u
                u = u + flux * rcoup_s[block, f, i]
                u_s[f, block * cycles + i] = u
                v_s[f, back * cycles + j] = v
                gain = gain + v
                v = v + gain * rcoup_s[back, f, j]
                carry[4 * f : 4 * f + 4] = [u, flux, v, gain]
        return tuple(carry)

    one, zero = jnp.float32(1.0), jnp.float32(0.0)
    last = lax.fori_loop(0, n_rad, chain, (one, -one, one, zero) * fluids)
    tile = (vertical, LANES)
    scale = [1.0 / jnp.full(tile, last[4 * f] + last[4 * f + 1], jnp.float32) for f in range(fluids)]

    offset = width * blocks[a] + cells[a]
    shift = offset % LANES
    base = 2 * tiles * n_az - offset // LANES
    weight = fracs[a]
    lane = lax.broadcasted_iota(jnp.int32, tile, 1)
    near_keep = lane >= shift
    far_keep = lane >= shift + 1
    far_shift = (shift + 1) % LANES

    def rotated_chip(f, t):
        near, far = [], []
        for j in range(-1, 2 * tiles):
            source = recv1[f][(base + (2 * tiles * t + j)) & (tiles * n_az - 1)]
            near.append(pltpu.roll(source, shift, 1))
            far.append(pltpu.roll(source, far_shift, 1))
        for j in range(2 * tiles):
            nearer = jnp.where(near_keep, near[j + 1], near[j])
            farther = jnp.where(far_keep, far[j + 1], far[j])
            send2[f][2 * t + j // tiles, j % tiles] = (1.0 - weight) * nearer + weight * farther

    def go_back(p):
        f, start, count = PIECES[p]
        part = pl.ds(start, count)
        if start == 0:
            arrived(recv1[f], p1_recv.at[f])

        def send_back(t):
            pltpu.make_async_remote_copy(
                src_ref=send2[f].at[t, part],
                dst_ref=recv2[f].at[a, part],
                send_sem=p2_send.at[p],
                recv_sem=p2_recv.at[p],
                device_id={"az": t},
                device_id_type=MESH,
            ).start()

        def give(step, carry):
            t = other_chip(step)
            if start == 0:
                rotated_chip(f, t)
            send_back(2 * t + core)
            send_back(2 * t + 1 - core)
            return carry

        lax.fori_loop(0, chips - 1, give, 0)
        if start == 0:
            rotated_chip(f, chip)
        send_back(2 * chip + 1 - core)
        pltpu.make_async_copy(send2[f].at[a, part], recv2[f].at[a, part], p2_recv.at[p]).start()

    first = k * cycles

    def share(p):
        f, start, count = PIECES[p]
        part = pl.ds(start, count)
        plane = (count, vertical, LANES)
        arrived(recv2[f].at[pl.ds(0, n_az), part], p2_recv.at[p])
        nothing = jnp.zeros(plane, jnp.float32)

        def add(n, sums):
            sums = list(sums)
            for j in range(8):
                i = 8 * n + j
                row = recv2[f][i, part]
                sums[j % 2] += u_s[f, first + i] * row
                sums[2 + j % 2] += v_s[f, first + i] * row
            return tuple(sums)

        sums = lax.fori_loop(0, cycles // 8, add, (nothing,) * 4, unroll=True)
        zsend[p][0] = scale[f] * (sums[0] + sums[1])
        zsend[p][1] = scale[f] * (sums[2] + sums[3])
        for step in range(1, n_rad):
            t = (k + step) % n_rad
            pltpu.make_async_remote_copy(
                src_ref=zsend[p].at[jnp.where(t > k, 0, 1)],
                dst_ref=zrecv[p].at[k],
                send_sem=z_send.at[p],
                recv_sem=z_recv.at[p],
                device_id={"rad": t},
                device_id_type=MESH,
            ).start()
        zrecv[p][k] = nothing

    def solve(p):
        f, start, count = PIECES[p]
        part = pl.ds(start, count)
        nothing = jnp.zeros((count, vertical, LANES), jnp.float32)

        def outward(i, total):
            total = total + u_s[f, first + i] * recv2[f][i, part]
            out[f, i, part] = v_s[f, first + i] * total
            return total

        lax.fori_loop(0, cycles, outward, nothing, unroll=8)

        def inward(n, total):
            i = cycles - 1 - n
            out[f, i, part] = scale[f] * (out[f, i, part] + u_s[f, first + i] * total)
            return total + v_s[f, first + i] * recv2[f][i, part]

        lax.fori_loop(0, cycles, inward, nothing, unroll=8)

    def finish(p):
        f, start, count = PIECES[p]
        part = pl.ds(start, count)
        arrived(zrecv[p].at[pl.ds(0, n_rad - 1)], z_recv.at[p])
        inner = jnp.zeros((count, vertical, LANES), jnp.float32)
        outer = inner
        for block in range(n_rad):
            sums = zrecv[p][block]
            inner = inner + jnp.where(block < k, sums, 0.0)
            outer = outer + jnp.where(block > k, sums, 0.0)

        if p == len(PIECES) - 1:
            edges[0] = inner
            edges[1] = outer
            return

        def add(i, carry):
            out[f, i, part] = out[f, i, part] + v_s[f, first + i] * inner + u_s[f, first + i] * outer
            return carry

        lax.fori_loop(0, cycles, add, 0, unroll=8)

    for p in range(len(PIECES)):
        if p >= AHEAD:
            share(p - AHEAD)
        go_back(p)
        if p >= AHEAD:
            solve(p - AHEAD)
            if p > AHEAD:
                finish(p - AHEAD - 1)
    for p in range(len(PIECES) - AHEAD, len(PIECES)):
        share(p)
        solve(p)
        if p > 0:
            finish(p - 1)

    def spell(i, carry):
        f = PIECES[-1][0]
        table[0, i] = jnp.full(tile, v_s[f, first + i], jnp.float32)
        table[1, i] = jnp.full(tile, u_s[f, first + i], jnp.float32)
        return carry

    lax.fori_loop(0, cycles, spell, 0, unroll=8)
    finish(len(PIECES) - 1)

    for f in range(fluids):
        arrived(recv1[f].at[pl.ds(0, tiles * (n_az - 1))], p1_send.at[f])
    for p, (f, start, count) in enumerate(PIECES):
        arrived(recv2[f].at[pl.ds(0, n_az - 1), pl.ds(start, count)], p2_send.at[p])
        arrived(zrecv[p].at[pl.ds(0, n_rad - 1)], z_send.at[p])


def store(held, edges, table, out, last, sem):
    f, start, count = PIECES[-1]
    cycles = held.shape[1]
    ready = [
        pltpu.make_async_copy(held.at[g, :, pl.ds(begin, n)], out.at[g, :, pl.ds(begin, n)], sem.at[s])
        for s, (g, begin, n) in enumerate(((0, 0, 4), (1, 0, 2)))
    ]
    for copy in ready:
        copy.start()
    inner, outer = edges[0], edges[1]

    def add(i, carry):
        last[i] = held[f, i, pl.ds(start, count)] + table[0, i] * inner + table[1, i] * outer
        return carry

    lax.fori_loop(0, cycles, add, 0, unroll=8)
    final = pltpu.make_async_copy(last, out.at[f, :, pl.ds(start, count)], sem.at[len(ready)])
    final.start()
    for copy in ready:
        copy.wait()
    final.wait()


def per_device(fields, cycle_blocks, cycle_cells, cycle_fracs, coupling):
    n_az, n_rad = lax.axis_size("az"), lax.axis_size("rad")
    fluids, cycles, vertical, width = fields.shape
    tiles = width // LANES
    ring = pltpu.VMEM((n_az, tiles, vertical, LANES), jnp.float32)
    flat = pltpu.VMEM((n_az * tiles, vertical, LANES), jnp.float32)
    pieces = len(PIECES)
    tiled = fields.reshape(fluids, cycles, vertical, tiles, LANES).transpose(0, 1, 3, 2, 4)
    operands = [tiled, cycle_blocks.reshape(cycles), cycle_cells, cycle_fracs, coupling]
    operands = [pltpu.with_memory_space_constraint(x, pltpu.HBM) for x in operands]
    every = (n_rad, fluids, cycles)
    evolved = pl.pallas_call(
        functools.partial(kernel, n_az, n_rad),
        out_shape=(
            pltpu.VMEM(tiled.shape, jnp.float32),
            pltpu.VMEM((2, PIECES[-1][2], vertical, LANES), jnp.float32),
            pltpu.VMEM((2, cycles, vertical, LANES), jnp.float32),
        ),
        in_specs=[pl.BlockSpec(memory_space=pltpu.HBM)] * 5,
        out_specs=(pl.BlockSpec(memory_space=pltpu.VMEM),) * 3,
        scratch_shapes=[flat] * 2 + [ring] * 4
        + [
            pltpu.VMEM(every, jnp.float32),
            pltpu.VMEM(every, jnp.float32),
            pltpu.SMEM(every, jnp.float32),
            pltpu.SMEM((fluids, n_rad * cycles), jnp.float32),
            pltpu.SMEM((fluids, n_rad * cycles), jnp.float32),
            pltpu.SMEM((cycles,), jnp.int32),
            pltpu.SMEM((cycles,), jnp.int32),
            pltpu.SMEM((cycles,), jnp.float32),
            pltpu.SemaphoreType.DMA((fluids,)),
            pltpu.SemaphoreType.DMA((fluids,)),
            pltpu.SemaphoreType.DMA((pieces,)),
            pltpu.SemaphoreType.DMA((pieces,)),
            pltpu.SemaphoreType.DMA((pieces,)),
            pltpu.SemaphoreType.DMA((pieces,)),
            pltpu.SemaphoreType.DMA,
            pltpu.SemaphoreType.DMA,
            pltpu.SemaphoreType.DMA((4,)),
        ]
        + [pltpu.VMEM((2, count, vertical, LANES), jnp.float32) for _, _, count in PIECES]
        + [pltpu.VMEM((n_rad, count, vertical, LANES), jnp.float32) for _, _, count in PIECES],
        compiler_params=pltpu.CompilerParams(
            collective_id=0, has_side_effects=True, vmem_limit_bytes=32 * 1024 * 1024
        ),
    )(*operands)
    evolved = pl.pallas_call(
        store,
        out_shape=pltpu.HBM(tiled.shape, jnp.float32),
        in_specs=[pl.BlockSpec(memory_space=pltpu.VMEM)] * 3,
        out_specs=pl.BlockSpec(memory_space=pltpu.HBM),
        scratch_shapes=[
            pltpu.VMEM((cycles, PIECES[-1][2], vertical, LANES), jnp.float32),
            pltpu.SemaphoreType.DMA((pieces,)),
        ],
    )(*[pltpu.with_memory_space_constraint(x, pltpu.VMEM) for x in evolved])
    return evolved.transpose(0, 1, 3, 2, 4).reshape(fields.shape)


def solution(mesh):
    return jax.shard_map(
        per_device,
        mesh=mesh,
        in_specs=(P(None, "rad", None, "az"), P("rad", None), P("rad"), P("rad"), P(None, "rad")),
        out_specs=P(None, "rad", None, "az"),
        check_vma=False,
    )
```

```python
import functools

import jax
import jax.numpy as jnp
from jax import lax
from jax.experimental import pallas as pl
from jax.experimental.pallas import tpu as pltpu
from jax.sharding import PartitionSpec as P

MESH = pl.DeviceIdType.MESH
LANES = 128
PIECES = ((0, 0, 2), (0, 2, 2), (1, 0, 2), (1, 2, 2))
AHEAD = 3


def arrived(part, sem):
    pltpu.make_async_copy(part, part, sem).wait()


def kernel(
    n_az,
    n_rad,
    fields,
    blocks_in,
    cells_in,
    fracs_in,
    coupling,
    out,
    recv1_0,
    recv1_1,
    send2_0,
    send2_1,
    recv2_0,
    recv2_1,
    coup_all,
    rcoup,
    rcoup_s,
    u_s,
    v_s,
    blocks,
    cells,
    fracs,
    p1_send,
    p1_recv,
    p2_send,
    p2_recv,
    z_send,
    z_recv,
    c_send,
    c_recv,
    a_sem,
    *z_buffers,
):
    recv1 = (recv1_0, recv1_1)
    send2 = (send2_0, send2_1)
    recv2 = (recv2_0, recv2_1)
    zsend, zrecv = z_buffers[: len(PIECES)], z_buffers[len(PIECES) :]
    fluids, cycles, tiles, vertical, _ = fields.shape
    width = tiles * LANES
    chips = n_az // 2
    side = 4
    a = lax.axis_index("az")
    k = lax.axis_index("rad")
    chip, core = a >> 1, a & 1

    def far_first(i):
        return 2 + 3 * i + 3 * (i * (i - 1) >> 1)

    def other_chip(step):
        turn = 1 - 2 * core
        x = ((chip >> 2) + turn * far_first(step >> 2)) & (side - 1)
        y = (chip + turn * far_first(step & (side - 1))) & (side - 1)
        return x * side + y

    barrier = pltpu.get_barrier_semaphore()
    small = [
        pltpu.make_async_copy(coupling, coup_all.at[k], a_sem.at[0]),
        pltpu.make_async_copy(blocks_in, blocks, a_sem.at[1]),
        pltpu.make_async_copy(cells_in, cells, a_sem.at[2]),
        pltpu.make_async_copy(fracs_in, fracs, a_sem.at[3]),
    ]
    for copy in small:
        copy.start()
    for step in range(1, n_rad):
        pl.semaphore_signal(barrier, inc=1, device_id={"rad": (k + step) % n_rad}, device_id_type=MESH)

    def greet(step, carry):
        t = other_chip(step)
        for c in range(2):
            pl.semaphore_signal(barrier, inc=1, device_id={"az": 2 * t + c}, device_id_type=MESH)
        return carry

    lax.fori_loop(0, chips - 1, greet, 0)
    pl.semaphore_signal(barrier, inc=1, device_id={"az": 2 * chip + 1 - core}, device_id_type=MESH)
    pl.semaphore_wait(barrier, n_az - 1 + n_rad - 1)

    for f in range(fluids):

        def send_cycle(t, f=f):
            pltpu.make_async_remote_copy(
                src_ref=fields.at[f, t],
                dst_ref=recv1[f].at[pl.ds(tiles * a, tiles)],
                send_sem=p1_send.at[f],
                recv_sem=p1_recv.at[f],
                device_id={"az": t},
                device_id_type=MESH,
            ).start()

        def spread(step, carry, send_cycle=send_cycle):
            t = other_chip(step)
            send_cycle(2 * t + core)
            send_cycle(2 * t + 1 - core)
            return carry

        pltpu.make_async_copy(fields.at[f, a], recv1[f].at[pl.ds(tiles * a, tiles)], p1_recv.at[f]).start()
        lax.fori_loop(0, chips - 1, spread, 0)
        send_cycle(2 * chip + 1 - core)
        if f == 0:
            for copy in small:
                copy.wait()
            for step in range(1, n_rad):
                pltpu.make_async_remote_copy(
                    src_ref=coup_all.at[k],
                    dst_ref=coup_all.at[k],
                    send_sem=c_send,
                    recv_sem=c_recv,
                    device_id={"rad": (k + step) % n_rad},
                    device_id_type=MESH,
                ).start()

    arrived(coup_all.at[pl.ds(0, n_rad - 1)], c_recv)
    arrived(coup_all.at[pl.ds(0, n_rad - 1)], c_send)
    rcoup[...] = 1.0 / coup_all[...]
    to_scalar = pltpu.make_async_copy(rcoup, rcoup_s, a_sem.at[0])
    to_scalar.start()
    to_scalar.wait()

    def chain(block, carry):
        carry = list(carry)
        back = n_rad - 1 - block
        for i in range(cycles):
            j = cycles - 1 - i
            for f in range(fluids):
                u, flux, v, gain = carry[4 * f : 4 * f + 4]
                flux = flux + u
                u = u + flux * rcoup_s[block, f, i]
                u_s[f, block * cycles + i] = u
                v_s[f, back * cycles + j] = v
                gain = gain + v
                v = v + gain * rcoup_s[back, f, j]
                carry[4 * f : 4 * f + 4] = [u, flux, v, gain]
        return tuple(carry)

    one, zero = jnp.float32(1.0), jnp.float32(0.0)
    last = lax.fori_loop(0, n_rad, chain, (one, -one, one, zero) * fluids)
    tile = (vertical, LANES)
    scale = [1.0 / jnp.full(tile, last[4 * f] + last[4 * f + 1], jnp.float32) for f in range(fluids)]

    offset = width * blocks[a] + cells[a]
    shift = offset % LANES
    base = 2 * tiles * n_az - offset // LANES
    weight = fracs[a]
    lane = lax.broadcasted_iota(jnp.int32, tile, 1)
    near_keep = lane >= shift
    far_keep = lane >= shift + 1
    far_shift = (shift + 1) % LANES

    def rotated_chip(f, t):
        near, far = [], []
        for j in range(-1, 2 * tiles):
            source = recv1[f][(base + (2 * tiles * t + j)) & (tiles * n_az - 1)]
            near.append(pltpu.roll(source, shift, 1))
            far.append(pltpu.roll(source, far_shift, 1))
        for j in range(2 * tiles):
            nearer = jnp.where(near_keep, near[j + 1], near[j])
            farther = jnp.where(far_keep, far[j + 1], far[j])
            send2[f][2 * t + j // tiles, j % tiles] = (1.0 - weight) * nearer + weight * farther

    def go_back(p):
        f, start, count = PIECES[p]
        part = pl.ds(start, count)
        if start == 0:
            arrived(recv1[f], p1_recv.at[f])

        def send_back(t):
            pltpu.make_async_remote_copy(
                src_ref=send2[f].at[t, part],
                dst_ref=recv2[f].at[a, part],
                send_sem=p2_send.at[p],
                recv_sem=p2_recv.at[p],
                device_id={"az": t},
                device_id_type=MESH,
            ).start()

        def give(step, carry):
            t = other_chip(step)
            if start == 0:
                rotated_chip(f, t)
            send_back(2 * t + core)
            send_back(2 * t + 1 - core)
            return carry

        lax.fori_loop(0, chips - 1, give, 0)
        if start == 0:
            rotated_chip(f, chip)
        send_back(2 * chip + 1 - core)
        pltpu.make_async_copy(send2[f].at[a, part], recv2[f].at[a, part], p2_recv.at[p]).start()

    first = k * cycles

    def share(p):
        f, start, count = PIECES[p]
        part = pl.ds(start, count)
        plane = (count, vertical, LANES)
        arrived(recv2[f].at[pl.ds(0, n_az), part], p2_recv.at[p])
        nothing = jnp.zeros(plane, jnp.float32)

        def add(n, sums):
            sums = list(sums)
            for j in range(8):
                i = 8 * n + j
                row = recv2[f][i, part]
                sums[j % 2] += u_s[f, first + i] * row
                sums[2 + j % 2] += v_s[f, first + i] * row
            return tuple(sums)

        sums = lax.fori_loop(0, cycles // 8, add, (nothing,) * 4, unroll=True)
        zsend[p][0] = scale[f] * (sums[0] + sums[1])
        zsend[p][1] = scale[f] * (sums[2] + sums[3])
        for step in range(1, n_rad):
            t = (k + step) % n_rad
            pltpu.make_async_remote_copy(
                src_ref=zsend[p].at[jnp.where(t > k, 0, 1)],
                dst_ref=zrecv[p].at[k],
                send_sem=z_send.at[p],
                recv_sem=z_recv.at[p],
                device_id={"rad": t},
                device_id_type=MESH,
            ).start()
        zrecv[p][k] = nothing

    def solve(p):
        f, start, count = PIECES[p]
        part = pl.ds(start, count)
        nothing = jnp.zeros((count, vertical, LANES), jnp.float32)

        def outward(i, total):
            total = total + u_s[f, first + i] * recv2[f][i, part]
            out[f, i, part] = v_s[f, first + i] * total
            return total

        lax.fori_loop(0, cycles, outward, nothing, unroll=8)

        def inward(n, total):
            i = cycles - 1 - n
            out[f, i, part] = scale[f] * (out[f, i, part] + u_s[f, first + i] * total)
            return total + v_s[f, first + i] * recv2[f][i, part]

        lax.fori_loop(0, cycles, inward, nothing, unroll=8)

    def finish(p):
        f, start, count = PIECES[p]
        part = pl.ds(start, count)
        arrived(zrecv[p].at[pl.ds(0, n_rad - 1)], z_recv.at[p])
        inner = jnp.zeros((count, vertical, LANES), jnp.float32)
        outer = inner
        for block in range(n_rad):
            sums = zrecv[p][block]
            inner = inner + jnp.where(block < k, sums, 0.0)
            outer = outer + jnp.where(block > k, sums, 0.0)

        def add(i, carry):
            out[f, i, part] = out[f, i, part] + v_s[f, first + i] * inner + u_s[f, first + i] * outer
            return carry

        lax.fori_loop(0, cycles, add, 0, unroll=8)

    for p in range(len(PIECES)):
        if p >= AHEAD:
            share(p - AHEAD)
        go_back(p)
        if p >= AHEAD:
            solve(p - AHEAD)
            if p > AHEAD:
                finish(p - AHEAD - 1)
    for p in range(len(PIECES) - AHEAD, len(PIECES)):
        share(p)
        solve(p)
        if p > 0:
            finish(p - 1)
    finish(len(PIECES) - 1)

    for f in range(fluids):
        arrived(recv1[f].at[pl.ds(0, tiles * (n_az - 1))], p1_send.at[f])
    for p, (f, start, count) in enumerate(PIECES):
        arrived(recv2[f].at[pl.ds(0, n_az - 1), pl.ds(start, count)], p2_send.at[p])
        arrived(zrecv[p].at[pl.ds(0, n_rad - 1)], z_send.at[p])


def per_device(fields, cycle_blocks, cycle_cells, cycle_fracs, coupling):
    n_az, n_rad = lax.axis_size("az"), lax.axis_size("rad")
    fluids, cycles, vertical, width = fields.shape
    tiles = width // LANES
    ring = pltpu.VMEM((n_az, tiles, vertical, LANES), jnp.float32)
    flat = pltpu.VMEM((n_az * tiles, vertical, LANES), jnp.float32)
    pieces = len(PIECES)
    tiled = fields.reshape(fluids, cycles, vertical, tiles, LANES).transpose(0, 1, 3, 2, 4)
    operands = [tiled, cycle_blocks.reshape(cycles), cycle_cells, cycle_fracs, coupling]
    operands = [pltpu.with_memory_space_constraint(x, pltpu.HBM) for x in operands]
    every = (n_rad, fluids, cycles)
    evolved = pl.pallas_call(
        functools.partial(kernel, n_az, n_rad),
        out_shape=pltpu.VMEM(tiled.shape, jnp.float32),
        in_specs=[pl.BlockSpec(memory_space=pltpu.HBM)] * 5,
        out_specs=pl.BlockSpec(memory_space=pltpu.VMEM),
        scratch_shapes=[flat] * 2 + [ring] * 4
        + [
            pltpu.VMEM(every, jnp.float32),
            pltpu.VMEM(every, jnp.float32),
            pltpu.SMEM(every, jnp.float32),
            pltpu.SMEM((fluids, n_rad * cycles), jnp.float32),
            pltpu.SMEM((fluids, n_rad * cycles), jnp.float32),
            pltpu.SMEM((cycles,), jnp.int32),
            pltpu.SMEM((cycles,), jnp.int32),
            pltpu.SMEM((cycles,), jnp.float32),
            pltpu.SemaphoreType.DMA((fluids,)),
            pltpu.SemaphoreType.DMA((fluids,)),
            pltpu.SemaphoreType.DMA((pieces,)),
            pltpu.SemaphoreType.DMA((pieces,)),
            pltpu.SemaphoreType.DMA((pieces,)),
            pltpu.SemaphoreType.DMA((pieces,)),
            pltpu.SemaphoreType.DMA,
            pltpu.SemaphoreType.DMA,
            pltpu.SemaphoreType.DMA((4,)),
        ]
        + [pltpu.VMEM((2, count, vertical, LANES), jnp.float32) for _, _, count in PIECES]
        + [pltpu.VMEM((n_rad, count, vertical, LANES), jnp.float32) for _, _, count in PIECES],
        compiler_params=pltpu.CompilerParams(
            collective_id=0, has_side_effects=True, vmem_limit_bytes=32 * 1024 * 1024
        ),
    )(*operands)
    return evolved.transpose(0, 1, 3, 2, 4).reshape(fields.shape)


def solution(mesh):
    return jax.shard_map(
        per_device,
        mesh=mesh,
        in_specs=(P(None, "rad", None, "az"), P("rad", None), P("rad"), P("rad"), P(None, "rad")),
        out_specs=P(None, "rad", None, "az"),
        check_vma=False,
    )
```
